32 devices in a mesh: pair: 8 (over z, x), aux: 4 (over y, core).
Axes of the slice: x: 2, y: 2, z: 4, core: 2. Of those that a mesh axis runs over, the one named last changes fastest.
Arguments:
- integrals: bfloat16 [3072, 8192], P(('aux', 'pair')), may hold values from -0.796875 to 0.796875
- metric: bfloat16 [3072, 3072], P('aux'), may hold values from -0.109375 to 0.109375
- occ_energy: float32 [8], replicated, may hold values from -1.5 to -0.3
- virt_energy: float32 [1024], replicated, may hold values from 0.3 to 3
- pair_table: int32 [16, 2], P('pair'), may hold values from 0 to 7, as said below
- pair_count: int32 [8], P('pair'), may hold values from 1 to 2, as said below
Outputs:
- grad_blocks: float32 [3072, 8192], P('aux', 'pair')
The draws below stay inside these ranges and needn't reach their ends.
Inputs may be any that keep to these rules, and one draw needn't show every extreme that they name: `pair_table`: occupied indices of the batch; slots beyond an owner's count hold valid but unused indices. `pair_count`: some owner holds exactly 2 listed pairs.
All inputs are finite; a program needn't handle non-finite values.
Results may differ from the reference program's by a relative error of at most 0.0028.
Values may be sent and summed in bfloat16 or wider, within the bound.
No kernel may reach another device: no remote copies, remote signals or barrier semaphores. Data moves between devices by JAX's collectives and lax.ppermute only.
A program may use at most 128 MiB of HBM per device.

```python
import jax
import jax.numpy as jnp
from jax import lax

NAUX = 3072
NVIRT = 1024
OCC = 8
CAP = 2
OWNERS = 8
SLOTS = 16
N_AUX = 4


def draw_pair_count(key, part):
    first_key, second_key = jax.random.split(jax.random.fold_in(key, 11))
    counts = jax.random.randint(first_key, (OWNERS,), 1, CAP + 1)
    busiest = jax.random.randint(second_key, (), 0, OWNERS)
    return jnp.where(jnp.arange(OWNERS) == busiest, CAP, counts).astype(jnp.int32)


def draw_pair_table(key, part):
    return jax.random.randint(jax.random.fold_in(key, 23), (SLOTS, 2), 0, OCC).astype(jnp.int32)


def block_scale(stream_key, extent, shards, low, largest):
    def one(axis_at, shards_of):
        steps = jax.random.uniform(jax.random.fold_in(jax.random.fold_in(stream_key, 6), axis_at), (shards_of,), jnp.float32, low / len(shards), largest / len(shards))
        return jnp.repeat(jnp.exp(steps), extent[axis_at] // shards_of).reshape((-1,) + (1,) * (len(extent) - axis_at - 1))

    level = one(*shards[0])
    for cut in shards[1:]:
        level = level * one(*cut)
    return level


def scatter_about(stream_key, shape, deviation, bound, cuts=(), kind=jnp.bfloat16):
    entries = jax.random.normal(stream_key, shape, jnp.float32) * deviation
    if len(cuts) > 0:
        entries = block_scale(stream_key, shape, cuts, -0.22, 0.18) * entries
    return jnp.clip(entries, min=-bound, max=bound).astype(kind)


def setup_inputs(seed: int = 0) -> dict:
    seeds = jax.random.split(jax.random.key(seed), 7)
    return {
        "integrals": scatter_about(seeds[0], (NAUX, OCC * NVIRT), 0.1, 0.796875, ((0, 32),)),
        "metric": scatter_about(seeds[1], (NAUX, NAUX), NAUX ** -0.5, 0.109375, ((0, 4),)),
        "occ_energy": jnp.clip(jax.random.uniform(seeds[2], (OCC,), jnp.float32, -1.5, -0.3), -1.5, -0.3),
        "virt_energy": jnp.clip(jax.random.uniform(seeds[3], (NVIRT,), jnp.float32, 0.3, 3.0), 0.3, 3.0),
        "pair_table": draw_pair_table(jax.random.fold_in(seeds[6], 71), 0),
        "pair_count": draw_pair_count(jax.random.fold_in(seeds[6], 71), 0),
    }


def add_row(gradient, row_values, index):
    current = lax.dynamic_index_in_dim(gradient, index, 1, keepdims=False)
    return lax.dynamic_update_index_in_dim(gradient, current + row_values, index, 1)


def reference(integrals, metric, occ_energy, virt_energy, pair_table, pair_count):
    slab = NAUX // N_AUX
    fitted = jnp.zeros((NAUX, OCC * NVIRT), jnp.float32)
    for piece in range(N_AUX):
        term = lax.dot_general(metric[piece * slab:(piece + 1) * slab], integrals[piece * slab:(piece + 1) * slab], (((0,), (0,)), ((), ())), preferred_element_type=jnp.float32)
        fitted = fitted + term
    fitted_b = fitted.astype(jnp.bfloat16).reshape(NAUX, OCC, NVIRT)
    living = (jnp.arange(CAP, dtype=jnp.int32)[None, :] < pair_count[:, None]).reshape(-1)

    def visit(slot, gradient):
        occ_left = pair_table[slot, 0].astype(jnp.int32)
        occ_right = pair_table[slot, 1].astype(jnp.int32)
        left = lax.dynamic_index_in_dim(fitted_b, occ_left, 1, keepdims=False)
        right = lax.dynamic_index_in_dim(fitted_b, occ_right, 1, keepdims=False)
        pair_ints = lax.dot_general(left, right, (((0,), (0,)), ((), ())), preferred_element_type=jnp.float32)
        denominator = virt_energy[:, None] + virt_energy[None, :] - occ_energy[occ_left] - occ_energy[occ_right]
        amplitude = (pair_ints / denominator).astype(jnp.bfloat16)
        to_left = lax.dot_general(right, amplitude, (((1,), (1,)), ((), ())), preferred_element_type=jnp.float32)
        to_right = jnp.dot(left, amplitude, preferred_element_type=jnp.float32)
        gradient = add_row(gradient, to_left, occ_left)
        return add_row(gradient, to_right, occ_right)

    def skip(slot, gradient):
        return gradient

    def step(slot, gradient):
        return lax.cond(living[slot], visit, skip, slot, gradient)

    gradient = lax.fori_loop(0, SLOTS, step, jnp.zeros((NAUX, OCC, NVIRT), jnp.float32))
    return gradient.reshape(NAUX, OCC * NVIRT)
```

```python
import functools

import jax
import jax.numpy as jnp
import numpy as np
from jax import lax
from jax.experimental import pallas as pl
from jax.experimental.pallas import tpu as pltpu
from jax.sharding import PartitionSpec as P

CORES = 2
RING = (0, 1, 3, 2)
CHUNKS = 2
VMEM = 56 * 1024 * 1024


class Layout:
    def __init__(self, mesh):
        self.n_pair = mesh.shape["pair"]
        self.n_aux = mesh.shape["aux"]
        self.nz = len(RING)
        self.nx = self.n_pair // self.nz
        self.ny = self.n_aux // CORES

    def pair_shift(self, s, t):
        return [
            (RING[r] * self.nx + x, RING[(r + s) % self.nz] * self.nx + (x + t) % self.nx)
            for r in range(self.nz)
            for x in range(self.nx)
        ]

    def y_shift(self, k):
        return [
            (y * CORES + c, (y + k) % self.ny * CORES + c)
            for y in range(self.ny)
            for c in range(CORES)
        ]

    def core_swap(self):
        return [(a, a ^ 1) for a in range(self.n_aux)]

    def inverse(self, g):
        return (-g[0] % self.nz, -g[1] % self.nx)

    def elements(self):
        return [(s, t) for s in range(self.nz) for t in range(self.nx)]


def to_pair(x, lay, s, t):
    return lax.ppermute(x, "pair", lay.pair_shift(s % lay.nz, t % lay.nx))


def to_y(x, lay, k):
    return lax.ppermute(x, "aux", lay.y_shift(k))


def to_core(x, lay):
    return lax.ppermute(x, "aux", lay.core_swap())


def products_kernel(entries, table, own, *rest):
    blocks, out = rest[:-1], rest[-1]
    w = own.shape[-1]

    def one(c, carry):
        i, j = table[0, c], table[1, c]
        for way, (l, r) in enumerate(((i, j), (j, i))):
            for e, (b, d) in enumerate(entries):
                if d == way:
                    out[c, e] = lax.dot_general(
                        own[l], blocks[b][r], (((0,), (0,)), ((), ())), preferred_element_type=jnp.float32
                    )
        return carry

    lax.fori_loop(0, table.shape[1], one, 0)


def products(table, own, blocks, entries):
    slots = table.shape[1]
    w = own.shape[-1]
    flops = 2 * slots * len(entries) * w * w * own.shape[1]
    vm = pl.BlockSpec(memory_space=pltpu.VMEM)
    return pl.pallas_call(
        functools.partial(products_kernel, entries),
        out_shape=jax.ShapeDtypeStruct((slots, len(entries), w, w), jnp.float32),
        in_specs=[pl.BlockSpec(memory_space=pltpu.SMEM)] + [vm] * (1 + len(blocks)),
        out_specs=vm,
        compiler_params=pltpu.CompilerParams(vmem_limit_bytes=VMEM),
        cost_estimate=pl.CostEstimate(flops=2 * flops, bytes_accessed=4 * slots * len(entries) * w * w, transcendentals=0),
        name="products",
    )(table, own, *blocks)


def gradient_kernel(where, n_blocks, table, *rest):
    blocks, weights = rest[:n_blocks], rest[n_blocks:-2]
    out, acc = rest[-2:]
    w = out.shape[-1]
    acc[...] = jnp.zeros_like(acc)

    def one(c, carry):
        i, j = table[0, c], table[1, c]
        for way, (l, r) in enumerate(((i, j), (j, i))):
            parts = [(blocks[b][r], weights[g][c, e]) for b, g, e in where[way]]
            if w % 128 == 0:
                parts = [(jnp.concatenate([x for x, _ in parts], axis=1), jnp.concatenate([y for _, y in parts], axis=0))]
            total = acc[l]
            for x, y in parts:
                total = total + jnp.dot(x, y, preferred_element_type=jnp.float32)
            acc[l] = total
        return carry

    lax.fori_loop(0, table.shape[1], one, 0)
    out[...] = acc[...].astype(out.dtype)


def gradient_of(table, blocks, weights, where):
    occ, rows, w = blocks[0].shape
    tile = 256 if rows % 256 == 0 else 128
    spec = pl.BlockSpec((occ, tile, w), lambda q: (0, q, 0))
    slots = table.shape[1]
    flops = 2 * 2 * slots * rows * w * w * len(blocks)
    return pl.pallas_call(
        functools.partial(gradient_kernel, where, len(blocks)),
        grid=(rows // tile,),
        out_shape=jax.ShapeDtypeStruct((occ, rows, w), jnp.bfloat16),
        in_specs=[pl.BlockSpec(memory_space=pltpu.SMEM)]
        + [spec] * len(blocks)
        + [pl.BlockSpec(memory_space=pltpu.VMEM)] * len(weights),
        out_specs=spec,
        scratch_shapes=[pltpu.VMEM((occ, tile, w), jnp.float32)],
        compiler_params=pltpu.CompilerParams(vmem_limit_bytes=VMEM),
        cost_estimate=pl.CostEstimate(flops=2 * flops, bytes_accessed=2 * occ * rows * w * len(blocks), transcendentals=0),
        name="gradient",
    )(table, *blocks, *weights)


def reduce_slots(x, lay, share):
    half = x.shape[0] // CORES
    x = x[:half] + to_core(x[half:], lay)
    total = x[:share]
    for k in range(1, lay.ny):
        total = total + to_y(x[k * share:(k + 1) * share], lay, k)
    return total


def gather_slots(x, lay):
    x = jnp.concatenate([x] + [to_y(x, lay, k) for k in range(1, lay.ny)], axis=0)
    return jnp.concatenate([x, to_core(x, lay)], axis=0)


def on_device(lay, integrals, metric, occ_energy, virt_energy, pair_table, pair_count):
    n_pair, n_aux, ny = lay.n_pair, lay.n_aux, lay.ny
    occ = occ_energy.shape[0]
    parts = n_pair // occ
    u = integrals.shape[1] // (n_pair * n_pair)
    w = parts * u
    slab = metric.shape[0]
    aux = lax.axis_index("aux")
    y, c = aux // CORES, aux % CORES
    pair = lax.axis_index("pair")
    z, x = pair // lay.nx, pair % lay.nx

    cap = pair_table.shape[0]
    listed = jnp.concatenate([pair_table, jnp.broadcast_to(pair_count, (cap, 1))], axis=1)
    listed = lax.all_gather(listed, "pair", axis=0, tiled=True)
    slots = listed.shape[0]
    share = slots // n_aux
    valid = jnp.arange(slots) % cap < listed[:, 2]
    grouped = listed[:, :2].reshape(n_aux, share, 2)

    def ordered(sign):
        owners = jnp.stack([(y + sign * k) % ny * CORES + (c ^ cc) for cc in range(CORES) for k in range(ny)])
        return grouped[owners].reshape(slots, 2).T

    scatter_table, gather_table = ordered(1), ordered(-1)
    mine = lax.dynamic_index_in_dim(grouped, aux, 0, keepdims=False)
    mine_valid = lax.dynamic_index_in_dim(valid.reshape(n_aux, share), aux, 0, keepdims=False)
    mine_shift = occ_energy[mine[:, 0]], occ_energy[mine[:, 1]]
    virt_of = virt_energy.reshape(parts, n_pair, u).transpose(1, 0, 2).reshape(n_pair, w)

    wide = slab * CORES

    def columns(k):
        return lax.dynamic_slice_in_dim(metric, (y + k) % ny * wide, wide, 1)

    near = jnp.concatenate([columns(0)] + [to_y(columns(k), lay, k) for k in range(1, ny)], axis=0)
    far = to_core(lax.dynamic_slice_in_dim(near, (1 - c) * slab, slab, 1), lay)
    near = lax.dynamic_slice_in_dim(near, c * slab, slab, 1)
    metric_t = jnp.concatenate([near, far], axis=0).T

    def fit(piece):
        wide_d = piece.shape[1] // (n_pair * u)
        got = lax.all_to_all(
            piece.reshape(piece.shape[0], wide_d, n_pair, u), "pair", split_axis=2, concat_axis=0, tiled=True
        ).reshape(slab, wide_d * u)
        got = jnp.concatenate([got] + [to_y(got, lay, k) for k in range(1, ny)], axis=0)
        got = jnp.concatenate([got, to_core(got, lay)], axis=0)
        fitted = jnp.dot(metric_t, got, preferred_element_type=jnp.float32).astype(jnp.bfloat16)
        return fitted.reshape(slab, wide_d // parts, w).transpose(1, 0, 2)

    cut = integrals.shape[1] // CHUNKS
    own = jnp.concatenate([fit(integrals[:, h * cut:(h + 1) * cut]) for h in range(CHUNKS)], axis=0)

    block = {(0, 0): own}
    for s in range(lay.nz):
        nxt = to_pair(block[s, 0], lay, 1, 0) if s + 1 < lay.nz else None
        for t in range(1, lay.nx):
            block[s, t] = to_pair(block[s, t - 1], lay, 0, 1)
        if nxt is not None:
            last = (s, lay.nx - 1)
            nxt, block[last] = lax.optimization_barrier((nxt, block[last]))
            block[s + 1, 0] = nxt

    firsts = [g for g in lay.elements() if g <= lay.inverse(g)]
    groups = [[g for g in firsts if g <= (1, 0)], [g for g in firsts if g > (1, 0)]]
    ring_at = jnp.asarray(np.argsort(RING))[z]
    own_virt = virt_of[pair]
    all_weights, place = [], ({}, {})
    for n_group, group in enumerate(groups):
        entries = []
        for b, g in enumerate(group):
            entries.append((b, 0))
            if g != lay.inverse(g):
                entries.append((b, 1))
        partial = products(scatter_table, own, [block[g] for g in group], tuple(entries))
        summed = reduce_slots(partial, lay, share)
        stack, keys = [], []
        for b, g in enumerate(group):
            source = jnp.asarray(RING)[(ring_at - g[0]) % lay.nz] * lay.nx + (x - g[1]) % lay.nx
            energy = own_virt[:, None] + virt_of[source][None, :]
            energy = energy[None] - mine_shift[0][:, None, None] - mine_shift[1][:, None, None]

            def amplitude(e):
                return jnp.where(mine_valid[:, None, None], summed[:, e] / energy, 0.0).astype(jnp.bfloat16)

            here = [amplitude(e) for e, (bb, _) in enumerate(entries) if bb == b]
            keys.append((g, 0))
            stack.append(here[0].transpose(0, 2, 1))
            back = lay.inverse(g)
            if g == (0, 0):
                keys.append((g, 1))
                stack.append(here[0])
            elif back == g:
                keys.append((g, 1))
                stack.append(to_pair(here[0], lay, -g[0], -g[1]))
            else:
                keys.append((g, 1))
                stack.append(here[1].transpose(0, 2, 1))
                got = to_pair(jnp.stack(here, axis=1), lay, -g[0], -g[1])
                keys += [(back, 1), (back, 0)]
                stack += [got[:, 0], got[:, 1]]
        all_weights.append(gather_slots(jnp.stack(stack, axis=1), lay))
        for e, (g, way) in enumerate(keys):
            place[way][g] = (n_group, e)

    order = lay.elements()
    where = tuple(tuple((b, *place[way][g]) for b, g in enumerate(order)) for way in (0, 1))
    gradient = gradient_of(gather_table, [block[g] for g in order], all_weights, where)
    gradient = gradient.reshape(occ, slab, parts, u).transpose(0, 2, 1, 3).reshape(n_pair, slab, u)
    home = lax.all_to_all(gradient, "pair", split_axis=0, concat_axis=0, tiled=True)
    return home.transpose(1, 0, 2).reshape(slab, n_pair * u).astype(jnp.float32)


def solution(mesh):
    placed = (P(("aux", "pair"), None), P("aux", None), P(), P(), P("pair", None), P("pair"))
    return jax.shard_map(
        functools.partial(on_device, Layout(mesh)), mesh=mesh, in_specs=placed, out_specs=P("aux", "pair"), check_vma=False
    )
```

```python
import functools

import jax
import jax.numpy as jnp
import numpy as np
from jax import lax
from jax.experimental import pallas as pl
from jax.experimental.pallas import tpu as pltpu
from jax.sharding import PartitionSpec as P

CORES = 2
RING = (0, 1, 3, 2)
HALVES = 2
HOME_CHUNKS = 1
PIECES = 2
EXTRA_ROWS = 16
VMEM = 56 * 1024 * 1024
F32 = jnp.float32
BF16 = jnp.bfloat16


class Layout:
    def __init__(self, mesh):
        self.n_pair = mesh.shape["pair"]
        self.n_aux = mesh.shape["aux"]
        self.nz = len(RING)
        self.nx = self.n_pair // self.nz
        self.ny = self.n_aux // CORES

    def pair_shift(self, s, t):
        return [
            (RING[r] * self.nx + x, RING[(r + s) % self.nz] * self.nx + (x + t) % self.nx)
            for r in range(self.nz)
            for x in range(self.nx)
        ]

    def y_shift(self, k, flip=0):
        return [
            (y * CORES + c, (y + k) % self.ny * CORES + (c ^ flip))
            for y in range(self.ny)
            for c in range(CORES)
        ]

    def core_swap(self):
        return [(a, a ^ 1) for a in range(self.n_aux)]

    def inverse(self, g):
        return (-g[0] % self.nz, -g[1] % self.nx)

    def elements(self):
        return [(s, t) for s in range(self.nz) for t in range(self.nx)]


def to_pair(x, lay, s, t):
    return lax.ppermute(x, "pair", lay.pair_shift(s % lay.nz, t % lay.nx))


def to_y(x, lay, k):
    return lax.ppermute(x, "aux", lay.y_shift(k))


def to_core(x, lay):
    return lax.ppermute(x, "aux", lay.core_swap())


def after(values, *done):
    return lax.optimization_barrier((tuple(values), done))[0]


WHOLE = pl.BlockSpec(memory_space=pltpu.VMEM)
SCALARS = pl.BlockSpec(memory_space=pltpu.SMEM)


def params():
    return pltpu.CompilerParams(vmem_limit_bytes=VMEM)


def cost(flops, moved):
    return pl.CostEstimate(flops=int(flops), bytes_accessed=int(moved), transcendentals=0)


def fit_kernel(places, starts, *rest):
    metrics, pieces, out = rest[:len(places)], rest[len(places):-1], rest[-1]
    w = out.shape[-1]
    total = None
    for metric, (source, start) in zip(metrics, places):
        depth = metric.shape[1]
        if start is None:
            piece = pieces[source][...]
        else:
            piece = pieces[source][pl.ds(pl.multiple_of(starts[start], depth), depth), :]
        term = jnp.dot(metric[...], piece, preferred_element_type=F32)
        total = term if total is None else total + term
    for i in range(out.shape[0]):
        out[i] = total[:, i * w:(i + 1) * w].astype(BF16)


def fit_more_kernel(places, so_far, *rest):
    del so_far
    fit_kernel(places, *rest)


def fit(metrics, places, starts, pieces, w, occ, part, so_far):
    rows = metrics[0].shape[0]
    wide = pieces[0].shape[1]
    depth = sum(metric.shape[1] for metric in metrics)
    tile = 256 if rows % 256 == 0 else 128
    given = [] if so_far is None else [so_far]
    return pl.pallas_call(
        functools.partial(fit_kernel if so_far is None else fit_more_kernel, places),
        grid=(rows // tile,),
        out_shape=jax.ShapeDtypeStruct((occ, rows, w), BF16),
        in_specs=[pl.BlockSpec(memory_space=pl.ANY)] * len(given)
        + [SCALARS]
        + [pl.BlockSpec((tile, metric.shape[1]), lambda q: (q, 0)) for metric in metrics]
        + [WHOLE] * len(pieces),
        out_specs=pl.BlockSpec((wide // w, tile, w), lambda q: (part, q, 0)),
        input_output_aliases={0: 0} if given else {},
        compiler_params=params(),
        cost_estimate=cost(2 * rows * depth * wide, 2 * (rows + wide) * depth),
        name="fit",
    )(*given, starts, *metrics, *pieces)


def spread(cat, blocks):
    w = blocks[0][0].shape[-1]
    for b, block in enumerate(blocks):
        at = 0
        for ref in block:
            n = ref.shape[0]
            cat[at:at + n, :, b * w:(b + 1) * w] = ref[...]
            at += n


def split(refs, counts):
    out, at = [], 0
    for n in counts:
        out.append(refs[at:at + n])
        at += n
    return out, refs[at:]


def products_kernel(n_blocks, n_both, n_chunks, table, own, *rest):
    blocks, chunks, (own_t, cat) = rest[:n_blocks], rest[n_blocks:n_blocks + n_chunks], rest[-2:]
    w = own_t.shape[1]
    spread(cat, [[ref] for ref in blocks])
    for i in range(own.shape[0]):
        own_t[i] = own[i].T
    for n, out in enumerate(chunks):
        share = out.shape[0]
        for c in range(share):
            i, j = table[0, n * share + c], table[1, n * share + c]
            first = jnp.dot(own_t[i], cat[j], preferred_element_type=F32)
            for e in range(n_blocks):
                out[c, e] = first[:, e * w:(e + 1) * w]
            if n_both > 0:
                second = jnp.dot(own_t[j], cat[i, :, :n_both * w], preferred_element_type=F32)
                for e in range(n_both):
                    out[c, n_blocks + e] = second[:, e * w:(e + 1) * w]


def products(table, n_chunks, own, blocks, n_both):
    slots = table.shape[1]
    occ, rows, w = own.shape
    entries = len(blocks) + n_both
    chunk = jax.ShapeDtypeStruct((slots // n_chunks, entries, w, w), F32)
    return pl.pallas_call(
        functools.partial(products_kernel, len(blocks), n_both, n_chunks),
        out_shape=(chunk,) * n_chunks,
        in_specs=[SCALARS] + [WHOLE] * (1 + len(blocks)),
        out_specs=(WHOLE,) * n_chunks,
        scratch_shapes=[pltpu.VMEM((occ, w, rows), BF16), pltpu.VMEM((occ, rows, len(blocks) * w), BF16)],
        compiler_params=params(),
        cost_estimate=cost(2 * slots * entries * w * w * rows, 4 * slots * entries * w * w),
        name="products",
    )(table, own, *blocks)


def amplitude_kernel(plan, n_terms, numbers, down, across, *rest):
    terms, weights, sent = rest[:n_terms], rest[n_terms], rest[n_terms + 1:]
    share = weights.shape[0]
    part = share // PIECES
    for s in range(share):
        left, right, live = numbers[0, s], numbers[1, s], numbers[2, s]
        for e, (block, flipped, plain, out, slot) in enumerate(plan):
            total = None
            for term in terms[s // part::PIECES]:
                value = term[s % part, e]
                total = value if total is None else total + value
            below = down[...] + across[block:block + 1, :] - left - right
            amp = jnp.where(live > 0, total / below, 0.0)
            weights[s, flipped] = amp.T.astype(BF16)
            if plain is not None:
                weights[s, plain] = amp.astype(BF16)
            if out is not None:
                sent[out][s, slot] = amp.astype(BF16)


def amplitudes(plan, numbers, down, across, terms, n_weights, sends):
    share, w = numbers.shape[1], terms[0].shape[-1]
    entries = len(plan)
    outs = [n_weights] + sends
    return pl.pallas_call(
        functools.partial(amplitude_kernel, plan, len(terms)),
        out_shape=tuple(jax.ShapeDtypeStruct((share, n, w, w), BF16) for n in outs),
        in_specs=[SCALARS] + [WHOLE] * (2 + len(terms)),
        out_specs=(WHOLE,) * len(outs),
        compiler_params=params(),
        cost_estimate=cost(share * entries * w * w * 10, share * entries * w * w * 8),
        name="amplitudes",
    )(numbers, down, across, *terms)


def gradient_kernel(where, counts, n_rounds, n_chunks, has_start, table, *rest):
    blocks, rest = split(rest, counts)
    rounds = [rest[g * n_chunks:(g + 1) * n_chunks] for g in range(n_rounds)]
    rest = rest[n_rounds * n_chunks:]
    if has_start:
        start, out, acc, cat = rest
        acc[...] = start[...]
    else:
        out, acc, cat = rest
        acc[...] = jnp.zeros_like(acc)
    w = out.shape[-1]
    spread(cat, blocks)
    share = rounds[0][0].shape[0]
    for chunk in range(n_chunks):

        for s in range(share):
            at = chunk * share + s
            i, j = table[0, at], table[1, at]
            for way, (l, r) in enumerate(((i, j), (j, i))):
                right = jnp.concatenate([rounds[g][chunk][s, e] for g, e in where[way]], axis=0)
                acc[l] += jnp.dot(cat[r], right, preferred_element_type=F32)
    out[...] = acc[...].astype(out.dtype)


def gradient(table, blocks, rounds, where, tile, first, tiles, start, kind):
    occ, rows, w = blocks[0][0].shape
    slots = table.shape[1]
    n_chunks = len(rounds[0])
    parts = [part for block in blocks for part in block]
    flat = [chunk for one in rounds for chunk in one]
    starts = [] if start is None else [start]
    return pl.pallas_call(
        functools.partial(
            gradient_kernel, where, [len(block) for block in blocks], len(rounds), n_chunks, start is not None
        ),
        grid=(tiles,),
        out_shape=jax.ShapeDtypeStruct((occ, tiles * tile, w), kind),
        in_specs=[SCALARS]
        + [pl.BlockSpec((part.shape[0], tile, w), lambda q: (0, q + first, 0)) for part in parts]
        + [WHOLE] * len(flat)
        + [pl.BlockSpec((occ, tile, w), lambda q: (0, q + first, 0))] * len(starts),
        out_specs=pl.BlockSpec((occ, tile, w), lambda q: (0, q, 0)),
        scratch_shapes=[pltpu.VMEM((occ, tile, w), F32), pltpu.VMEM((occ, tile, len(blocks) * w), BF16)],
        compiler_params=params(),
        cost_estimate=cost(4 * slots * tiles * tile * w * w * len(blocks), 2 * occ * tiles * tile * w * len(blocks)),
        name="gradient",
    )(table, *parts, *flat, *starts)


def arrange_kernel(given, out):
    u = given.shape[-1]
    for p in range(given.shape[0]):
        out[:, p * u:(p + 1) * u] = given[p].astype(F32)


def arrange(given):
    n, rows, u = given.shape
    tile = 128 if rows % 128 == 0 else rows
    return pl.pallas_call(
        arrange_kernel,
        grid=(rows // tile,),
        out_shape=jax.ShapeDtypeStruct((rows, n * u), F32),
        in_specs=[pl.BlockSpec((n, tile, u), lambda q: (0, q, 0))],
        out_specs=pl.BlockSpec((tile, n * u), lambda q: (q, 0)),
        compiler_params=params(),
        cost_estimate=cost(0, 6 * n * rows * u),
        name="arrange",
    )(given)


def gather_slots(x, lay):
    here = [x] + [to_y(x, lay, k) for k in range(1, lay.ny)]
    return here + [to_core(v, lay) for v in here]


def on_device(lay, integrals, metric, occ_energy, virt_energy, pair_table, pair_count):
    n_pair, n_aux, ny, nz, nx = lay.n_pair, lay.n_aux, lay.ny, lay.nz, lay.nx
    occ = occ_energy.shape[0]
    parts = n_pair // occ
    u = integrals.shape[1] // (n_pair * n_pair)
    w = parts * u
    slab = metric.shape[0]
    aux = lax.axis_index("aux")
    y, c = aux // CORES, aux % CORES
    pair = lax.axis_index("pair")
    z, x = pair // nx, pair % nx

    step = integrals.shape[1] // HALVES
    wide_d = step // (n_pair * u)
    rows = integrals.shape[0]

    def regroup(piece):
        got = lax.all_to_all(
            piece.reshape(piece.shape[0], wide_d, n_pair, u), "pair", split_axis=2, concat_axis=0, tiled=True
        )
        return got.reshape(slab // rows, piece.shape[0], wide_d * u)

    cap = pair_table.shape[0]
    slots = n_pair * cap
    listed = jnp.concatenate([pair_table.reshape(-1), pair_count]).astype(BF16)
    listed = jnp.pad(listed, (0, u - listed.shape[0]))
    listed = jnp.broadcast_to(listed, (EXTRA_ROWS, step // u, u)).reshape(EXTRA_ROWS, step)

    def slot_tables(listed):
        listed = listed.astype(jnp.int32)
        pairs = listed[:, :2 * cap].reshape(slots, 2)
        live = (jnp.arange(cap) < listed[:, 2 * cap:2 * cap + 1]).astype(jnp.int32).reshape(slots, 1)
        grouped = jnp.concatenate([pairs, live], axis=1).reshape(n_aux, share, 3)

        def ordered(sign):
            owners = jnp.stack([(y + sign * k) % ny * CORES + (c ^ cc) for cc in range(CORES) for k in range(ny)])
            return grouped[owners].reshape(slots, 3).T

        mine = lax.dynamic_index_in_dim(grouped, aux, 0, keepdims=False)
        numbers = jnp.stack([occ_energy[mine[:, 0]], occ_energy[mine[:, 1]], mine[:, 2].astype(F32)])
        return ordered(1), ordered(-1), numbers

    share = slots // n_aux
    ring_at = jnp.asarray(np.argsort(RING))[z]
    virt_of = virt_energy.reshape(parts, n_pair, u).transpose(1, 0, 2).reshape(n_pair, w)
    own_virt = virt_of[pair][:, None]

    def source(g):
        return jnp.asarray(RING)[(ring_at - g[0]) % nz] * nx + (x - g[1]) % nx

    across = {g: virt_of[source(g)] for g in lay.elements()}

    cut = slab // nx
    starts = jnp.stack([(x - t) % nx * cut for t in range(nx)])
    metrics, places = [], []

    def columns(k, cc):
        return ((y + k) % ny * CORES + (c ^ cc)) * slab

    metrics.append(lax.dynamic_slice_in_dim(metric, columns(0, 0), slab, 1).T)
    crossed = to_core(lax.dynamic_slice_in_dim(metric, columns(0, 1), slab, 1), lay)
    places += [(0, None), (ny, None)]
    parts_y = {}
    for k in range(1, ny):
        for cc in range(CORES):
            part = lax.dynamic_slice(metric, (x * cut, columns(k, cc)), (cut, slab))
            parts_y[k, cc] = part
    first, = after((jnp.concatenate([integrals[:, :step], listed], axis=0),), *parts_y.values())
    parts_y = {key: lax.ppermute(part, "aux", lay.y_shift(*key)) for key, part in parts_y.items()}
    first = regroup(first)
    scatter_table, gather_table, numbers = slot_tables(first[:, rows, :u])
    first = first[:, :rows].reshape(slab, -1)
    second, *arrived = after([integrals[:, step:], *parts_y.values()], first)
    second = regroup(second).reshape(slab, -1)
    swapped = []
    keys_y = list(parts_y)
    arrived = jnp.stack(arrived)
    for t in range(nx):
        if t > 0:
            arrived = to_pair(arrived, lay, 0, 1)
        swapped += [arrived[n] for n in range(len(keys_y))]
        places += [(cc * ny + k, t) for k, cc in keys_y]

    def from_aux(part):
        there = [part] + [to_y(part, lay, k) for k in range(1, ny)]
        return there + [to_core(v, lay) for v in there]

    there = from_aux(first)
    ready = after((second, crossed, scatter_table, gather_table, numbers, *across.values()), *there[:ny])
    second, crossed, scatter_table, gather_table, numbers = ready[:5]
    across = dict(zip(across, ready[5:]))
    metrics.append(crossed.T)
    metrics += [part.T for part in swapped]
    own = fit(metrics, tuple(places), starts, there, w, occ, 0, None)
    own = fit(metrics, tuple(places), starts, from_aux(second), w, occ, 1, own)

    block = {(0, 0): [own]}

    def ring(s, *done):
        here = block[s, 0][0]
        if s < nz - 1:
            if done:
                here, = after((here,), *done)
            block[s + 1, 0] = [to_pair(here, lay, 1, 0)]
            for t in range(1, nx):
                here = to_pair(here, lay, 0, 1)
                block[s, t] = [here]
            return [block[s + 1, 0][0]] + [block[s, t][0] for t in range(1, nx)]
        half = occ // HALVES
        here, other = after((here, block[s - 1, nx - 1][0]), *done)
        for t in range(1, nx - 1):
            here = to_pair(here, lay, 0, 1)
            block[s, t] = [here]
        block[s, nx - 1] = [to_pair(here[:half], lay, 0, 1), to_pair(other[half:], lay, 1, 0)]
        return block[s, nx - 1]

    firsts = [g for g in lay.elements() if g <= lay.inverse(g)]
    stages = [[] for _ in range(nz)]
    for s, t in firsts:
        stages[s if t == 0 else s + 1].append((s, t))
    last = nz - 1
    rounds, pending, place = [], [], ({}, {})

    def collect(values):
        for e, (g, way) in enumerate([key for _, keys in values for key in keys]):
            place[way][g] = (len(rounds), e)
        arrays = [v for v, _ in values]
        rounds.append(gather_slots(arrays[0] if len(arrays) == 1 else jnp.concatenate(arrays, axis=1), lay))

    def sums(n, *done):
        both = [g for g in stages[n] if g != lay.inverse(g) or n == last]
        stage = both + [g for g in stages[n] if g not in both]
        here, = after((own,), *done) if done else (own,)
        chunks = products(scatter_table, n_aux * PIECES, here, [block[g][0] for g in stage], len(both))
        got = [to_core(v, lay) for v in chunks[ny * PIECES:]]
        terms = [chunks[:PIECES], got[:PIECES]]
        for k in range(1, ny):
            there = slice(k * PIECES, (k + 1) * PIECES)
            terms.append([to_y(near + far, lay, k) for near, far in zip(chunks[there], got[there])])
        terms = [piece for term in terms for piece in term]
        return stage, both, terms

    def weigh(stage, both, terms):
        rows_of = jnp.stack([across[g] for g in stage])
        entries = [(b, 0) for b in range(len(stage))] + [(b, 1) for b in range(len(both))]
        keys = [(g, way) for g in stage for way in range(2 if g in both or g == (0, 0) else 1)]
        plan, sends, out_of = [], [], {}
        for b, way in entries:
            g = stage[b]
            flipped, plain, out, slot = keys.index((g, way)), None, None, None
            if g == (0, 0):
                plain = keys.index((g, 1))
            elif g not in both or lay.inverse(g) != g:
                if g not in out_of:
                    out_of[g] = len(sends)
                    sends.append(0)
                out = out_of[g]
                slot = sends[out]
                sends[out] += 1
            plan.append((b, flipped, plain, out, slot))
        weights, *sent = amplitudes(tuple(plan), numbers, own_virt, rows_of, terms, len(keys), sends)
        arrived = []
        for g, out in out_of.items():
            back = lay.inverse(g)
            value = to_pair(sent[out], lay, -g[0], -g[1])
            arrived.append((value, [(g, 1)] if back == g else [(back, 1), (back, 0)]))
        return (weights, keys), arrived

    def only(weights, which):
        values, keys = weights
        at = [e for e, (g, _) in enumerate(keys) if g in which]
        if len(at) == len(keys):
            return weights
        return values[:, at[0]:at[-1] + 1], [keys[e] for e in at]

    def part(which, tile, first, tiles, start, kind):
        used = sorted({place[way][g][0] for g in which for way in (0, 1)})
        where = tuple(tuple((used.index(place[way][g][0]), place[way][g][1]) for g in which) for way in (0, 1))
        return gradient(
            gather_table, [block[g] for g in which], [rounds[r] for r in used], where, tile, first, tiles, start, kind
        )

    moved = ring(0)
    weights0, _ = weigh(*sums(0))
    collect([weights0])
    moved = ring(1, *moved, *rounds[0])
    weights1, arrived1 = weigh(*sums(1))
    collect([weights1])
    moved = ring(2, *moved, *[v for v, _ in arrived1])
    stage2 = sums(2, weights1[0])
    collect(arrived1)
    weights2, arrived2 = weigh(*stage2)
    collect([only(weights2, stage2[1])])
    moved = ring(3, *moved, *rounds[1], *rounds[2], *[v for v, _ in arrived2])
    stage3 = sums(3, weights2[0])
    rest2 = [g for g in stage2[0] if g not in stage2[1]]
    collect(arrived2 + [only(weights2, rest2)])

    def there(g):
        return all(g in place[way] and place[way][g][0] <= 3 for way in (0, 1))

    early = [g for g in lay.elements() if there(g)]
    late = [g for g in lay.elements() if g not in early]
    total = part(early, slab // 2, 0, 2, None, F32)
    weights3, arrived3 = weigh(stage3[0], stage3[1], after(stage3[2], *moved, total))
    collect([weights3])
    if arrived3:
        collect(arrived3)
    tile = slab // HOME_CHUNKS
    home = []
    for q in range(HOME_CHUNKS):
        rows = part(late, tile, q, 1, total, BF16)
        rows = rows.reshape(occ, tile, parts, u).transpose(0, 2, 1, 3).reshape(n_pair, tile, u)
        rows = lax.all_to_all(rows, "pair", split_axis=0, concat_axis=0, tiled=True)
        home.append(rows)
    return arrange(home[0]) if len(home) == 1 else jnp.concatenate([arrange(rows) for rows in home], axis=0)


def solution(mesh):
    placed = (P(("aux", "pair"), None), P("aux", None), P(), P(), P("pair", None), P("pair"))
    return jax.shard_map(
        functools.partial(on_device, Layout(mesh)), mesh=mesh, in_specs=placed, out_specs=P("aux", "pair"), check_vma=False
    )
```

```python
import functools

import jax
import jax.numpy as jnp
import numpy as np
from jax import lax
from jax.experimental import pallas as pl
from jax.experimental.pallas import tpu as pltpu
from jax.sharding import PartitionSpec as P

CORES = 2
RING = (0, 1, 3, 2)
HALVES = 2
PIECES = 2
EXTRA_ROWS = 16
VMEM = 56 * 1024 * 1024
F32 = jnp.float32
BF16 = jnp.bfloat16


class Layout:
    def __init__(self, mesh):
        self.n_pair = mesh.shape["pair"]
        self.n_aux = mesh.shape["aux"]
        self.nz = len(RING)
        self.nx = self.n_pair // self.nz
        self.ny = self.n_aux // CORES

    def pair_shift(self, s, t):
        return [
            (RING[r] * self.nx + x, RING[(r + s) % self.nz] * self.nx + (x + t) % self.nx)
            for r in range(self.nz)
            for x in range(self.nx)
        ]

    def y_shift(self, k, flip=0):
        return [
            (y * CORES + c, (y + k) % self.ny * CORES + (c ^ flip))
            for y in range(self.ny)
            for c in range(CORES)
        ]

    def core_swap(self):
        return [(a, a ^ 1) for a in range(self.n_aux)]

    def inverse(self, g):
        return (-g[0] % self.nz, -g[1] % self.nx)

    def elements(self):
        return [(s, t) for s in range(self.nz) for t in range(self.nx)]


def to_pair(x, lay, s, t):
    return lax.ppermute(x, "pair", lay.pair_shift(s % lay.nz, t % lay.nx))


def to_y(x, lay, k):
    return lax.ppermute(x, "aux", lay.y_shift(k))


def to_core(x, lay):
    return lax.ppermute(x, "aux", lay.core_swap())


def after(values, *done):
    return lax.optimization_barrier((tuple(values), tuple(done)))[0]


WHOLE = pl.BlockSpec(memory_space=pltpu.VMEM)
SCALARS = pl.BlockSpec(memory_space=pltpu.SMEM)


def params():
    return pltpu.CompilerParams(vmem_limit_bytes=VMEM)


def cost(flops, moved):
    return pl.CostEstimate(flops=int(flops), bytes_accessed=int(moved), transcendentals=0)


def fit_kernel(places, starts, *rest):
    metrics, pieces, out = rest[:len(places)], rest[len(places):-1], rest[-1]
    w = out.shape[-1]
    total = None
    for metric, (source, start) in zip(metrics, places):
        depth = metric.shape[1]
        if start is None:
            piece = pieces[source][...]
        else:
            piece = pieces[source][pl.ds(pl.multiple_of(starts[start], depth), depth), :]
        term = jnp.dot(metric[...], piece, preferred_element_type=F32)
        total = term if total is None else total + term
    for i in range(out.shape[0]):
        out[i] = total[:, i * w:(i + 1) * w].astype(BF16)


def fit_more_kernel(places, so_far, *rest):
    del so_far
    fit_kernel(places, *rest)


def fit(metrics, places, starts, pieces, w, occ, part, so_far):
    rows = metrics[0].shape[0]
    wide = pieces[0].shape[1]
    depth = sum(metric.shape[1] for metric in metrics)
    tile = 256 if rows % 256 == 0 else 128
    given = [] if so_far is None else [so_far]
    return pl.pallas_call(
        functools.partial(fit_kernel if so_far is None else fit_more_kernel, places),
        grid=(rows // tile,),
        out_shape=jax.ShapeDtypeStruct((occ, rows, w), BF16),
        in_specs=[pl.BlockSpec(memory_space=pl.ANY)] * len(given)
        + [SCALARS]
        + [pl.BlockSpec((tile, metric.shape[1]), lambda q: (q, 0)) for metric in metrics]
        + [WHOLE] * len(pieces),
        out_specs=pl.BlockSpec((wide // w, tile, w), lambda q: (part, q, 0)),
        input_output_aliases={0: 0} if given else {},
        compiler_params=params(),
        cost_estimate=cost(2 * rows * depth * wide, 2 * (rows + wide) * depth),
        name="fit",
    )(*given, starts, *metrics, *pieces)


def spread(cat, blocks):
    w = blocks[0][0].shape[-1]
    for b, block in enumerate(blocks):
        at = 0
        for ref in block:
            n = ref.shape[0]
            cat[at:at + n, :, b * w:(b + 1) * w] = ref[...]
            at += n


def split(refs, counts):
    out, at = [], 0
    for n in counts:
        out.append(refs[at:at + n])
        at += n
    return out, refs[at:]


def products_kernel(counts, n_both, n_chunks, table, own, *rest):
    blocks, rest = split(rest, counts)
    chunks, (own_t, cat) = rest[:n_chunks], rest[-2:]
    n_blocks = len(blocks)
    w = own_t.shape[1]
    spread(cat, blocks)
    for i in range(own.shape[0]):
        own_t[i] = own[i].T
    for n, out in enumerate(chunks):
        share = out.shape[0]
        for c in range(share):
            i, j = table[0, n * share + c], table[1, n * share + c]
            first = jnp.dot(own_t[i], cat[j], preferred_element_type=F32)
            for e in range(n_blocks):
                out[c, e] = first[:, e * w:(e + 1) * w]
            if n_both > 0:
                second = jnp.dot(own_t[j], cat[i, :, :n_both * w], preferred_element_type=F32)
                for e in range(n_both):
                    out[c, n_blocks + e] = second[:, e * w:(e + 1) * w]


def products(table, n_chunks, own, blocks, n_both):
    slots = table.shape[1]
    occ, rows, w = own.shape
    entries = len(blocks) + n_both
    parts = [part for block in blocks for part in block]
    chunk = jax.ShapeDtypeStruct((slots // n_chunks, entries, w, w), F32)
    return pl.pallas_call(
        functools.partial(products_kernel, [len(block) for block in blocks], n_both, n_chunks),
        out_shape=(chunk,) * n_chunks,
        in_specs=[SCALARS] + [WHOLE] * (1 + len(parts)),
        out_specs=(WHOLE,) * n_chunks,
        scratch_shapes=[pltpu.VMEM((occ, w, rows), BF16), pltpu.VMEM((occ, rows, len(blocks) * w), BF16)],
        compiler_params=params(),
        cost_estimate=cost(2 * slots * entries * w * w * rows, 4 * slots * entries * w * w),
        name="products",
    )(table, own, *parts)


def amplitude_kernel(plan, n_terms, numbers, down, across, *rest):
    terms, weights, sent = rest[:n_terms], rest[n_terms], rest[n_terms + 1:]
    share = weights.shape[0]
    part = share // PIECES
    for s in range(share):
        left, right, live = numbers[0, s], numbers[1, s], numbers[2, s]
        for e, (block, flipped, plain, out, slot) in enumerate(plan):
            total = None
            for term in terms[s // part::PIECES]:
                value = term[s % part, e]
                total = value if total is None else total + value
            below = down[...] + across[block:block + 1, :] - left - right
            amp = jnp.where(live > 0, total / below, 0.0)
            weights[s, flipped] = amp.T.astype(BF16)
            if plain is not None:
                weights[s, plain] = amp.astype(BF16)
            if out is not None:
                sent[out][s, slot] = amp.astype(BF16)


def amplitudes(plan, numbers, down, across, terms, n_weights, sends):
    share, w = numbers.shape[1], terms[0].shape[-1]
    entries = len(plan)
    outs = [n_weights] + sends
    return pl.pallas_call(
        functools.partial(amplitude_kernel, plan, len(terms)),
        out_shape=tuple(jax.ShapeDtypeStruct((share, n, w, w), BF16) for n in outs),
        in_specs=[SCALARS] + [WHOLE] * (2 + len(terms)),
        out_specs=(WHOLE,) * len(outs),
        compiler_params=params(),
        cost_estimate=cost(share * entries * w * w * 10, share * entries * w * w * 8),
        name="amplitudes",
    )(numbers, down, across, *terms)


def gradient_kernel(where, counts, n_rounds, n_chunks, has_start, table, *rest):
    blocks, rest = split(rest, counts)
    rounds = [rest[g * n_chunks:(g + 1) * n_chunks] for g in range(n_rounds)]
    rest = rest[n_rounds * n_chunks:]
    if has_start:
        start, out, acc, cat = rest
        acc[...] = start[...]
    else:
        out, acc, cat = rest
        acc[...] = jnp.zeros_like(acc)
    w = out.shape[-1]
    spread(cat, blocks)
    share = rounds[0][0].shape[0]
    for chunk in range(n_chunks):

        for s in range(share):
            at = chunk * share + s
            i, j = table[0, at], table[1, at]
            for way, (l, r) in enumerate(((i, j), (j, i))):
                right = jnp.concatenate([rounds[g][chunk][s, e] for g, e in where[way]], axis=0)
                acc[l] += jnp.dot(cat[r], right, preferred_element_type=F32)
    out[...] = acc[...].astype(out.dtype)


def gradient(table, blocks, rounds, where, tile, first, tiles, start, kind):
    occ, rows, w = blocks[0][0].shape
    slots = table.shape[1]
    n_chunks = len(rounds[0])
    parts = [part for block in blocks for part in block]
    flat = [chunk for one in rounds for chunk in one]
    starts = [] if start is None else [start]
    return pl.pallas_call(
        functools.partial(
            gradient_kernel, where, [len(block) for block in blocks], len(rounds), n_chunks, start is not None
        ),
        grid=(tiles,),
        out_shape=jax.ShapeDtypeStruct((occ, tiles * tile, w), kind),
        in_specs=[SCALARS]
        + [pl.BlockSpec((part.shape[0], tile, w), lambda q: (0, q + first, 0)) for part in parts]
        + [WHOLE] * len(flat)
        + [pl.BlockSpec((occ, tile, w), lambda q: (0, q + first, 0))] * len(starts),
        out_specs=pl.BlockSpec((occ, tile, w), lambda q: (0, q, 0)),
        scratch_shapes=[pltpu.VMEM((occ, tile, w), F32), pltpu.VMEM((occ, tile, len(blocks) * w), BF16)],
        compiler_params=params(),
        cost_estimate=cost(4 * slots * tiles * tile * w * w * len(blocks), 2 * occ * tiles * tile * w * len(blocks)),
        name="gradient",
    )(table, *parts, *flat, *starts)


def arrange_kernel(given, out):
    u = given.shape[-1]
    for p in range(given.shape[0]):
        out[:, p * u:(p + 1) * u] = given[p].astype(F32)


def arrange(given):
    n, rows, u = given.shape
    tile = rows // 2
    return pl.pallas_call(
        arrange_kernel,
        grid=(rows // tile,),
        out_shape=jax.ShapeDtypeStruct((rows, n * u), F32),
        in_specs=[pl.BlockSpec((n, tile, u), lambda q: (0, q, 0))],
        out_specs=pl.BlockSpec((tile, n * u), lambda q: (q, 0)),
        compiler_params=params(),
        cost_estimate=cost(0, 6 * n * rows * u),
        name="arrange",
    )(given)


def gather_slots(x, lay):
    here = [x] + [to_y(x, lay, k) for k in range(1, lay.ny)]
    return here + [to_core(v, lay) for v in here]


def on_device(lay, integrals, metric, occ_energy, virt_energy, pair_table, pair_count):
    n_pair, n_aux, ny, nz, nx = lay.n_pair, lay.n_aux, lay.ny, lay.nz, lay.nx
    occ = occ_energy.shape[0]
    parts = n_pair // occ
    u = integrals.shape[1] // (n_pair * n_pair)
    w = parts * u
    slab = metric.shape[0]
    aux = lax.axis_index("aux")
    y, c = aux // CORES, aux % CORES
    pair = lax.axis_index("pair")
    z, x = pair // nx, pair % nx

    step = integrals.shape[1] // HALVES
    wide_d = step // (n_pair * u)
    rows = integrals.shape[0]

    def by_owner(piece):
        piece = piece.reshape(piece.shape[0], wide_d, n_pair, u).transpose(2, 0, 1, 3)
        return piece.reshape(n_pair, piece.shape[1], wide_d * u)

    def regroup(piece):
        return lax.all_to_all(piece, "pair", split_axis=0, concat_axis=0, tiled=True)

    cap = pair_table.shape[0]
    slots = n_pair * cap
    listed = jnp.concatenate([pair_table.reshape(-1), pair_count]).astype(BF16)
    listed = jnp.pad(listed, (0, u - listed.shape[0]))
    listed = jnp.broadcast_to(listed, (EXTRA_ROWS, step // u, u)).reshape(EXTRA_ROWS, step)

    def slot_tables(listed):
        listed = listed.astype(jnp.int32)
        pairs = listed[:, :2 * cap].reshape(slots, 2)
        live = (jnp.arange(cap) < listed[:, 2 * cap:2 * cap + 1]).astype(jnp.int32).reshape(slots, 1)
        grouped = jnp.concatenate([pairs, live], axis=1).reshape(n_aux, share, 3)

        def ordered(sign):
            owners = jnp.stack([(y + sign * k) % ny * CORES + (c ^ cc) for cc in range(CORES) for k in range(ny)])
            return grouped[owners].reshape(slots, 3).T

        mine = lax.dynamic_index_in_dim(grouped, aux, 0, keepdims=False)
        numbers = jnp.stack([occ_energy[mine[:, 0]], occ_energy[mine[:, 1]], mine[:, 2].astype(F32)])
        return ordered(1), ordered(-1), numbers

    share = slots // n_aux
    ring_at = jnp.asarray(np.argsort(RING))[z]
    virt_of = virt_energy.reshape(parts, n_pair, u).transpose(1, 0, 2).reshape(n_pair, w)
    own_virt = virt_of[pair][:, None]

    def source(g):
        return jnp.asarray(RING)[(ring_at - g[0]) % nz] * nx + (x - g[1]) % nx

    across = {g: virt_of[source(g)] for g in lay.elements()}

    cut = slab // nx
    starts = jnp.stack([(x - t) % nx * cut for t in range(nx)])
    metrics, places = [], []

    def columns(k, cc):
        return ((y + k) % ny * CORES + (c ^ cc)) * slab

    metrics.append(lax.dynamic_slice_in_dim(metric, columns(0, 0), slab, 1).T)
    crossed = to_core(lax.dynamic_slice_in_dim(metric, columns(0, 1), slab, 1), lay)
    places += [(0, None), (ny, None)]
    parts_y = [
        lax.dynamic_slice(metric, (x * cut, (y + k) % ny * CORES * slab), (cut, CORES * slab)) for k in range(1, ny)
    ]
    first = by_owner(jnp.concatenate([integrals[:, :step], listed], axis=0))
    parts_y = [to_y(part, lay, k) for k, part in enumerate(parts_y, 1)]
    raw = first = regroup(first)
    scatter_table, gather_table, numbers = slot_tables(first[:, rows, :u])
    first = first[:, :rows].reshape(slab, -1)
    second, = after([by_owner(integrals[:, step:])], raw)
    second = regroup(second).reshape(slab, -1)
    first, *arrived = after([first, *parts_y])
    arrived = jnp.stack(arrived)
    for t in range(nx):
        if t > 0:
            arrived = to_pair(arrived, lay, 0, 1)
        for cc in range(CORES):
            here = lax.dynamic_slice_in_dim(arrived, (c ^ cc) * slab, slab, 2)
            if cc == 1:
                here = to_core(here, lay)
            swapped = [here[k - 1] for k in range(1, ny)]
            metrics += [part.T for part in swapped]
            places += [(cc * ny + k, t) for k in range(1, ny)]

    def from_aux(part):
        there = [part] + [to_y(part, lay, k) for k in range(1, ny)]
        return there + [to_core(v, lay) for v in there]

    there = from_aux(first)
    ready = after((second, crossed, scatter_table, gather_table, numbers, *across.values()), *there[:ny])
    second, crossed, scatter_table, gather_table, numbers = ready[:5]
    across = dict(zip(across, ready[5:]))
    metrics.insert(1, crossed.T)
    own = fit(metrics, tuple(places), starts, there, w, occ, 0, None)
    own = fit(metrics, tuple(places), starts, from_aux(second), w, occ, 1, own)

    block = {(0, 0): [own]}

    half = occ // HALVES

    def along(here, s, t_first, t_end, out):
        for t in range(t_first, t_end):
            here = to_pair(here, lay, 0, 1)
            block[s, t] = [here]
            out.append(here)
        return here

    def both_ways(s, done):
        here, other = block[s, 0][0], block[s - 1, nx - 1][-1]
        moved = []
        here, other = after((here, other), *done)
        here = along(here, s, 1, nx - 1, moved)
        block[s, nx - 1] = [to_pair(here[:half], lay, 0, 1), to_pair(other[-half:], lay, 1, 0)]
        return moved + block[s, nx - 1]

    def ring(s, x_too, *done):
        here = block[s, 0][0]
        if done:
            here, = after((here,), *done)
        block[s + 1, 0] = [to_pair(here, lay, 1, 0)]
        moved = [block[s + 1, 0][0]]
        if x_too:
            along(here, s, 1, nx, moved)
        return moved

    firsts = [g for g in lay.elements() if g <= lay.inverse(g)]
    stages = [[] for _ in range(nz)]
    for s, t in firsts:
        stages[s if t == 0 else s + 1].append((s, t))
    last = nz - 1
    rounds, pending, place = [], [], ({}, {})

    def collect(values):
        for e, (g, way) in enumerate([key for _, keys in values for key in keys]):
            place[way][g] = (len(rounds), e)
        arrays = [v for v, _ in values]
        rounds.append(gather_slots(arrays[0] if len(arrays) == 1 else jnp.concatenate(arrays, axis=1), lay))

    def sums(n, done=(), hold=()):
        both = [g for g in stages[n] if g != lay.inverse(g) or n == last]
        stage = both + [g for g in stages[n] if g not in both]
        here, = after((own,), *done) if done else (own,)
        chunks = products(scatter_table, n_aux * PIECES, here, [block[g] for g in stage], len(both))
        got = [to_core(v, lay) for v in chunks[ny * PIECES:]]
        terms, sends = [chunks[:PIECES], got[:PIECES]], []
        for k in range(1, ny):
            there = slice(k * PIECES, (k + 1) * PIECES)
            going = [near + far for near, far in zip(chunks[there], got[there])]
            if hold:
                going = after(going, *hold)
            sends += going
            terms.append([to_y(value, lay, k) for value in going])
        terms = [piece for term in terms for piece in term]
        return (stage, both, terms), sends

    def weigh(stage, both, terms):
        rows_of = jnp.stack([across[g] for g in stage])
        entries = [(b, 0) for b in range(len(stage))] + [(b, 1) for b in range(len(both))]
        keys = [(g, way) for g in stage for way in range(2 if g in both or g == (0, 0) else 1)]
        plan, sends, out_of = [], [], {}
        for b, way in entries:
            g = stage[b]
            flipped, plain, out, slot = keys.index((g, way)), None, None, None
            if g == (0, 0):
                plain = keys.index((g, 1))
            elif g not in both or lay.inverse(g) != g:
                if g not in out_of:
                    out_of[g] = len(sends)
                    sends.append(0)
                out = out_of[g]
                slot = sends[out]
                sends[out] += 1
            plan.append((b, flipped, plain, out, slot))
        weights, *sent = amplitudes(tuple(plan), numbers, own_virt, rows_of, terms, len(keys), sends)
        return (weights, keys), [(sent[out], g) for g, out in out_of.items()]

    def exchange(sent, *done):
        arrived = []
        for value, g in sent:
            if done:
                value, = after((value,), *done)
            back = lay.inverse(g)
            value = to_pair(value, lay, -g[0], -g[1])
            arrived.append((value, [(g, 1)] if back == g else [(back, 1), (back, 0)]))
        return arrived

    def part(which, tile, first, tiles, start, kind):
        used = sorted({place[way][g][0] for g in which for way in (0, 1)})
        where = tuple(tuple((used.index(place[way][g][0]), place[way][g][1]) for g in which) for way in (0, 1))
        return gradient(
            gather_table, [block[g] for g in which], [rounds[r] for r in used], where, tile, first, tiles, start, kind
        )

    def only(weights, which):
        values, keys = weights
        at = [e for e, (g, _) in enumerate(keys) if g in which]
        if len(at) == len(keys):
            return weights
        return values[:, at[0]:at[-1] + 1], [keys[e] for e in at]

    moved = ring(0, True)
    stage0, _ = sums(0)
    weights0, _ = weigh(*stage0)
    collect([weights0])
    moved = ring(1, True, *moved, *rounds[0])
    stage1, _ = sums(1)
    weights1, sent1 = weigh(*stage1)
    collect([weights1])
    arrived1 = exchange(sent1)
    moved = ring(2, True, *moved, *[v for v, _ in arrived1])
    stage2, _ = sums(2, [weights1[0]])
    collect(arrived1)
    weights2, sent2 = weigh(*stage2)
    arrived2 = exchange(sent2)
    collect([only(weights2, stage2[1])])
    stage3, sends3 = sums(3, [weights2[0]])
    moved = both_ways(3, [*moved, *rounds[1], *rounds[2], *[v for v, _ in arrived2], *sends3])
    rest2 = [g for g in stage2[0] if g not in stage2[1]]
    arrived2 = [(after((v,), *stage3[2])[0], keys) for v, keys in arrived2]
    collect(arrived2 + [only(weights2, rest2)])

    def known(g, n):
        return all(g in place[way] and place[way][g][0] < n for way in (0, 1))

    early = [g for g in lay.elements() if known(g, 4)]
    late = [g for g in lay.elements() if g not in early]
    total = part(early, slab // 2, 0, 2, None, F32)
    weights3, sent3 = weigh(stage3[0], stage3[1], after(stage3[2], total, *moved))
    collect([weights3])
    if sent3:
        collect(exchange(sent3))
    rows = part(late, slab // 2, 0, 2, total, BF16)
    rows = rows.reshape(occ, slab, parts, u).transpose(0, 2, 1, 3).reshape(n_pair, slab, u)
    return arrange(lax.all_to_all(rows, "pair", split_axis=0, concat_axis=0, tiled=True))


def solution(mesh):
    placed = (P(("aux", "pair"), None), P("aux", None), P(), P(), P("pair", None), P("pair"))
    return jax.shard_map(
        functools.partial(on_device, Layout(mesh)), mesh=mesh, in_specs=placed, out_specs=P("aux", "pair"), check_vma=False
    )
```
